256 devices in a mesh: band: 4 (over x), region: 64 (over z, y, core).
Axes of the slice: x: 4, y: 4, z: 8, core: 2. Of those that a mesh axis runs over, the one named last changes fastest.
Arguments:
- fields: float32 [65536, 512], P(('band', 'region')), may hold values from -6 to 6
- send_list: int32 [4, 64, 4, 2], replicated, may hold values from -1 to 1, as said below
- departure: int32 [16, 65536], P(None, ('band', 'region')), may hold values from 0 to 1279, as said below
- hweight: float32 [16, 65536], P(None, ('band', 'region')), may hold values from -0.2 to 0.5
- base_level: int32 [128, 65536], P(None, ('band', 'region')), may hold values from 1 to 125
- vweight: float32 [4, 128, 65536], P(None, None, ('band', 'region')), may hold values from -0.25 to 0.75
- vertical_op: float32 [128, 128], replicated, may hold values from -0.4 to 2, as said below
Outputs:
- level_shards: float32 [512, 65536], P('region', 'band')
The draws below stay inside these ranges and needn't reach their ends.
Inputs may be any that keep to these rules, and one draw needn't show every extreme that they name: send_list[b, r, d] names distinct block numbers of device (b, r), each block being 128 consecutive points of it; a list holds 1 to 2 numbers followed by -1 in the remaining entries, and in every draw some region's lists are all full. departure[c, p] indexes the extended rows of point p's device: below 256 the device's own point, else 256 + d * 2 * 128 + s for row s of part d; only rows delivered by an existing neighbour from a list entry that is not -1 are named. vertical_op[k, l] is zero where k and l differ by more than 2.
All inputs are finite; a program needn't handle non-finite values.
Results may differ from the reference program's by a relative error of at most 0.0003.
Values sent between devices are 32-bit elements; how exact they have to be, the bound alone decides.
A program may use at most 64 MiB of HBM per device.

```python
import jax
import jax.numpy as jnp
from jax import lax

LEV = 128
P_DEV = 256
BLK = 128
STENCIL = 16
HB = 2
FL = 512
NPTS = 65536
N_BAND = 4
N_REGION = 64


def halo_counts(key):
    count_key, star_key = jax.random.split(jax.random.fold_in(key, 11))
    counts = jax.random.randint(count_key, (N_BAND, N_REGION, 4), 1, HB + 1)
    star_region = jax.random.randint(star_key, (), 0, N_REGION)
    region_ids = jnp.arange(N_REGION)[None, :, None]
    counts = jnp.where(region_ids == star_region, HB, counts)
    return (counts, star_region)


def draw_send_list(key, part):
    counts, star_region = halo_counts(key)
    order_keys = jax.random.split(jax.random.fold_in(key, 23), N_BAND * N_REGION * 4)
    orders = jax.vmap(lambda one_key: jax.random.permutation(one_key, P_DEV // BLK))(order_keys)
    orders = orders[:, :HB].reshape(N_BAND, N_REGION, 4, HB)
    slot_ids = jnp.arange(HB)[None, None, None, :]
    return jnp.where(slot_ids < counts[..., None], orders, -1).astype(jnp.int32)


def draw_departure(key, part):
    counts, star_region = halo_counts(key)
    band_ids = jnp.arange(N_BAND)[:, None]
    from_prev_band = jnp.where(band_ids > 0, jnp.roll(counts[:, :, 0], 1, axis=0), 0)
    from_next_band = jnp.where(band_ids < N_BAND - 1, jnp.roll(counts[:, :, 1], -1, axis=0), 0)
    from_prev_region = jnp.roll(counts[:, :, 2], 1, axis=1)
    from_next_region = jnp.roll(counts[:, :, 3], -1, axis=1)
    received = jnp.stack([from_prev_band, from_next_band, from_prev_region, from_next_region], axis=0)
    draw_keys = jax.random.split(jax.random.fold_in(key, 37), 3)
    grid_shape = (STENCIL, N_BAND, N_REGION, P_DEV)
    own_pick = jax.random.randint(draw_keys[0], grid_shape, 0, P_DEV)
    choose = jax.random.randint(draw_keys[1], grid_shape, 0, 8)
    side_pick = jnp.minimum(choose, 3)
    side_count = jnp.zeros(grid_shape, jnp.int32)
    for direction in range(4):
        side_count = side_count + jnp.where(side_pick == direction, received[direction][None, :, :, None], 0)
    slot_limit = jnp.maximum(side_count, 1) * BLK
    slot_pick = jax.random.randint(draw_keys[2], grid_shape, 0, slot_limit)
    use_halo = (choose < 4) & (side_count > 0)
    source_ids = jnp.where(use_halo, P_DEV + side_pick * (HB * BLK) + slot_pick, own_pick)
    source_ids = source_ids.at[0, 0, (star_region - 1) % N_REGION, 0].set(P_DEV + 4 * HB * BLK - 1)
    source_ids = source_ids.at[1, 0, 0, 0].set(0)
    return source_ids.reshape(STENCIL, N_BAND * N_REGION * P_DEV).astype(jnp.int32)


def draw_vertical_op(key, part):
    diag_key, spread_key = jax.random.split(jax.random.fold_in(key, 5))
    diagonal = jax.random.uniform(diag_key, (LEV,), jnp.float32, 1.0, 2.0)
    spread = jax.random.uniform(spread_key, (LEV, LEV), jnp.float32, -0.4, 0.4)
    level_ids = jnp.arange(LEV)
    distance = jnp.abs(level_ids[:, None] - level_ids[None, :])
    on_diagonal = diagonal[:, None] * jnp.ones((1, LEV), jnp.float32)
    return jnp.where(distance == 0, on_diagonal, jnp.where(distance <= 2, spread, 0.0)).astype(jnp.float32)


def with_ends(drawn, rng, low, largest):
    longest = drawn.shape.index(max(drawn.shape))
    spots = []
    for shift in (0, 1):
        where = [jax.random.randint(jax.random.fold_in(rng, axis), (), 0, length) for axis, length in enumerate(drawn.shape)]
        where[longest] = (where[longest] + shift) % drawn.shape[longest]
        spots.append(tuple(where))
    return drawn.at[spots[0]].set(low).at[spots[1]].set(largest)


def block_levels(own_key, shape, cuts, least, top_value):
    def one(dim, blocks):
        steps = jax.random.uniform(jax.random.fold_in(jax.random.fold_in(own_key, 6), dim), (blocks,), jnp.float32, least / len(cuts), top_value / len(cuts))
        return jnp.repeat(jnp.exp(steps), shape[dim] // blocks).reshape((-1,) + (1,) * (len(shape) - dim - 1))

    loudness = one(*cuts[0])
    for cut in cuts[1:]:
        loudness = loudness * one(*cut)
    return loudness


def scatter_about(key, extent, scale, reach, shards=(), kind=jnp.bfloat16):
    entries = scale * jax.random.normal(key, extent, jnp.float32)
    if shards:
        entries = entries * block_levels(key, extent, shards, -0.22, 0.18)
    return jnp.clip(entries, -reach, reach).astype(kind)


def setup_inputs(seed: int = 0) -> dict:
    key_list = jax.random.split(jax.random.key(seed), 8)
    return {
        "fields": scatter_about(key_list[0], (NPTS, FL), 1.0, 6.0, ((0, 256),), jnp.float32),
        "send_list": draw_send_list(jax.random.fold_in(key_list[7], 71), 0),
        "departure": draw_departure(jax.random.fold_in(key_list[7], 71), 0),
        "hweight": jnp.clip(-0.2 + 0.7 * jax.random.uniform(key_list[3], (STENCIL, NPTS), jnp.float32) ** block_levels(key_list[3], (STENCIL, NPTS), ((1, 256),), -0.2, 0.2), -0.2, 0.5),
        "base_level": with_ends(jax.random.randint(key_list[4], (LEV, NPTS), 1, LEV - 2), jax.random.fold_in(key_list[4], 1), 1, (LEV - 2) - 1).astype(jnp.int32),
        "vweight": jnp.clip(-0.25 + 1.0 * jax.random.uniform(key_list[5], (4, LEV, NPTS), jnp.float32) ** block_levels(key_list[5], (4, LEV, NPTS), ((2, 256),), -0.2, 0.2), -0.25, 0.75),
        "vertical_op": draw_vertical_op(jax.random.fold_in(key_list[7], 71), 0),
    }


exact_mode = lax.Precision.HIGHEST


def pack_blocks(block_table, block_list):
    safe_list = jnp.maximum(block_list, 0)
    picked = jnp.take(block_table, safe_list, axis=0)
    keeping = (block_list >= 0)[:, None, None]
    picked = jnp.where(keeping, picked, jnp.zeros((), picked.dtype))
    return picked.reshape(-1, picked.shape[-1])


def column_update(extended, depart_block, hweight_block, base_block, vweight_block, vertical_op):
    stencil_len, point_count = depart_block.shape
    width_all = extended.shape[1]
    levels = vertical_op.shape[0]
    fields_count = width_all // levels
    picked = jnp.take(extended, depart_block.reshape(-1), axis=0).reshape(stencil_len, point_count, width_all)
    horizontal = jnp.sum(hweight_block[:, :, None] * picked, axis=0)
    stacked = jnp.transpose(horizontal).reshape(fields_count, levels, point_count)
    interpolated = jnp.zeros(stacked.shape, jnp.float32)
    for offset in range(4):
        chosen = jnp.broadcast_to((base_block + (offset - 1))[None, :, :], stacked.shape)
        picked_levels = jnp.take_along_axis(stacked, chosen, axis=1)
        interpolated = interpolated + vweight_block[offset][None, :, :] * picked_levels
    operated = jnp.einsum("kl,flp->fkp", vertical_op, interpolated, precision=exact_mode)
    return operated.reshape(width_all, point_count)


def reference(fields, send_list, departure, hweight, base_level, vweight, vertical_op):
    width_all = fields.shape[1]
    block_count = P_DEV // BLK
    step_points = min(256, P_DEV)

    def device_blocks(device_id):
        start_row = (device_id * P_DEV).astype(jnp.int32)
        return lax.dynamic_slice_in_dim(fields, start_row, P_DEV, 0).reshape(block_count, BLK, width_all)

    def one_device(device_id):
        band_id = device_id // N_REGION
        region_id = device_id % N_REGION
        prev_band = jnp.maximum(band_id - 1, 0)
        next_band = jnp.minimum(band_id + 1, N_BAND - 1)
        prev_region = (region_id - 1) % N_REGION
        next_region = (region_id + 1) % N_REGION
        from_north = pack_blocks(device_blocks(prev_band * N_REGION + region_id), send_list[prev_band, region_id, 0])
        from_north = jnp.where(band_id > 0, from_north, jnp.zeros((), from_north.dtype))
        from_south = pack_blocks(device_blocks(next_band * N_REGION + region_id), send_list[next_band, region_id, 1])
        from_south = jnp.where(band_id < N_BAND - 1, from_south, jnp.zeros((), from_south.dtype))
        from_west = pack_blocks(device_blocks(band_id * N_REGION + prev_region), send_list[band_id, prev_region, 2])
        from_east = pack_blocks(device_blocks(band_id * N_REGION + next_region), send_list[band_id, next_region, 3])
        own_rows = device_blocks(device_id).reshape(P_DEV, width_all)
        extended = jnp.concatenate([own_rows, from_north, from_south, from_west, from_east], axis=0)
        base_col = (device_id * P_DEV).astype(jnp.int32)

        def one_step(step_id):
            first_col = (base_col + step_id * step_points).astype(jnp.int32)
            return column_update(
                extended,
                lax.dynamic_slice_in_dim(departure, first_col, step_points, 1),
                lax.dynamic_slice_in_dim(hweight, first_col, step_points, 1),
                lax.dynamic_slice_in_dim(base_level, first_col, step_points, 1),
                lax.dynamic_slice_in_dim(vweight, first_col, step_points, 2),
                vertical_op)

        pieces = lax.map(one_step, jnp.arange(P_DEV // step_points, dtype=jnp.int32))
        return jnp.transpose(pieces, (1, 0, 2)).reshape(width_all, P_DEV)

    results = lax.map(one_device, jnp.arange(N_BAND * N_REGION, dtype=jnp.int32))
    return jnp.transpose(results, (1, 0, 2)).reshape(width_all, N_BAND * N_REGION * P_DEV)
```

```python
import functools

import jax
import jax.numpy as jnp
from jax import lax
from jax.experimental import pallas as pl
from jax.experimental.pallas import tpu as pltpu
from jax.sharding import PartitionSpec as P

MESH = pl.DeviceIdType.MESH
LEV = 128
LANES = 128
FAR = 1 << 20
F32, BF16 = jnp.float32, jnp.bfloat16
NT = (((1,), (1,)), ((), ()))


def halves(x):
    high = x.astype(BF16)
    return high, (x - high.astype(F32)).astype(BF16)


def kernel(
    bands, regions, fields, lists, departure, hweight, base_level, vweight, vertical_op, out,
    own, halo, lists_s, dep_v, hw_v, base_v, vw_v, vop_v, dep_t, hw_t, w_f32, w_hi, w_lo, e_cat, base_t, vw_t, made,
    in_sem, halo_send, halo_recv, own_sem, send_sem, recv_sem,
):
    b, r = lax.axis_index("band"), lax.axis_index("region")
    points = fields.shape[0]
    n_fields = fields.shape[1] // LEV
    group = regions // n_fields
    rows = LEV // group
    east, west = lax.rem(r + 1, regions), lax.rem(r + regions - 1, regions)

    loads = [
        pltpu.make_async_copy(src, dst, in_sem.at[i])
        for i, (src, dst) in enumerate(
            [(lists, lists_s), (departure, dep_v), (hweight, hw_v), (base_level, base_v), (vweight, vw_v), (vertical_op, vop_v), (fields, own)]
        )
    ]
    for load in loads:
        load.start()

    barrier = pltpu.get_barrier_semaphore()

    def greet(band, region):
        pl.semaphore_signal(barrier, inc=1, device_id=(band, region), device_id_type=MESH)

    @pl.when(b > 0)
    def _():
        greet(b - 1, r)

    @pl.when(b < bands - 1)
    def _():
        greet(b + 1, r)

    def greet_region(i, carry):
        greet(b, lax.rem(r + i, regions))
        return carry

    lax.fori_loop(1, regions, greet_region, 0)
    pl.semaphore_wait(barrier, regions - 1 + jnp.minimum(b, 1) + jnp.minimum(bands - 1 - b, 1))

    def offset(t):
        return lax.rem(2 + t * (t + 1) // 2, n_fields)

    def field_of(region, t):
        return lax.rem(region // group + offset(t), n_fields)

    def halo_copy(t, d, band, region):
        column = pl.multiple_of(field_of(region, t) * LEV, LEV)
        return pltpu.make_async_remote_copy(
            src_ref=fields.at[:, pl.ds(column, LEV)],
            dst_ref=halo.at[t, d],
            send_sem=halo_send.at[t, d],
            recv_sem=halo_recv.at[t, d],
            device_id=(band, region),
            device_id_type=MESH,
        )

    def send_halo(t, carry):
        @pl.when(b < bands - 1)
        def _():
            halo_copy(t, 0, b + 1, r).start()

        @pl.when(b > 0)
        def _():
            halo_copy(t, 1, b - 1, r).start()

        halo_copy(t, 2, b, east).start()
        halo_copy(t, 3, b, west).start()
        return carry

    lax.fori_loop(0, n_fields, send_halo, 0)

    def blank(d):
        def one(t, carry):
            halo[t, d] = jnp.zeros(halo.shape[2:], F32)
            return carry

        lax.fori_loop(0, n_fields, one, 0)

    @pl.when(b == 0)
    def _():
        blank(0)

    @pl.when(b == bands - 1)
    def _():
        blank(1)

    for load in loads:
        load.wait()

    blocks = points // LANES
    bases = [i * LANES for i in range(blocks)]
    before, after = jnp.maximum(b - 1, 0), jnp.minimum(b + 1, bands - 1)
    for d, (band, region) in enumerate([(before, r), (after, r), (b, west), (b, east)]):
        first, second = (lists_s[band * 4 + d, e, region] for e in range(2))
        part = points + d * points
        for block in range(blocks):
            bases.append(jnp.where(first == block, part, jnp.where(second == block, part + LANES, FAR)))

    dep_t[...] = jnp.transpose(dep_v[...])
    hw_t[...] = jnp.transpose(hw_v[...])
    stencil = dep_v.shape[0]

    def weigh(i, carry):
        rows_i = pl.ds(pl.multiple_of(i * 8, 8), 8)
        dep, hw = dep_t[rows_i, :], hw_t[rows_i, :]
        deps = [jnp.broadcast_to(dep[:, c : c + 1], (8, LANES)) for c in range(stencil)]
        hws = [jnp.broadcast_to(hw[:, c : c + 1], (8, LANES)) for c in range(stencil)]
        lane = lax.broadcasted_iota(jnp.int32, (8, LANES), 1)
        for j, base in enumerate(bases):
            target = lane + base
            total = jnp.where(deps[0] == target, hws[0], 0.0)
            for c in range(1, stencil):
                total = total + jnp.where(deps[c] == target, hws[c], 0.0)
            w_f32[rows_i, j * LANES : (j + 1) * LANES] = total
        return carry

    lax.fori_loop(0, points // 8, weigh, 0)

    def split(i, carry):
        rows_i = pl.ds(pl.multiple_of(i * 16, 16), 16)
        w_hi[rows_i, :], w_lo[rows_i, :] = halves(w_f32[rows_i, :])
        return carry

    lax.fori_loop(0, points // 16, split, 0)

    base_t[...] = jnp.transpose(base_v[...])
    for m in range(4):
        vw_t[m] = jnp.transpose(vw_v[m])
    v_hi, v_lo = halves(vop_v[...])
    v_cat = jnp.concatenate([v_hi, v_hi], axis=1)

    def one_field(t, carry):
        f = field_of(r, t)
        column = pl.multiple_of(f * LEV, LEV)
        e_cat[:points, :LEV], e_cat[:points, LEV:] = halves(own[:, pl.ds(column, LEV)])

        @pl.when(b > 0)
        def _():
            halo_copy(t, 0, b, r).wait_recv()

        @pl.when(b < bands - 1)
        def _():
            halo_copy(t, 1, b, r).wait_recv()

        halo_copy(t, 2, b, r).wait_recv()
        halo_copy(t, 3, b, r).wait_recv()
        for d in range(4):
            part = slice((d + 1) * points, (d + 2) * points)
            e_cat[part, :LEV], e_cat[part, LEV:] = halves(halo[t, d])
        both = jnp.dot(w_hi[...], e_cat[...], preferred_element_type=F32)
        rest = jnp.dot(w_lo[...], e_cat[:, :LEV], preferred_element_type=F32)
        horizontal = both[:, :LEV] + both[:, LEV:] + rest
        mixed = jnp.zeros((points, LEV), F32)
        for m in range(4):
            picked = jnp.take_along_axis(horizontal, base_t[...] + (m - 1), axis=1, mode="promise_in_bounds")
            mixed = mixed + vw_t[m] * picked
        i_hi, i_lo = halves(mixed)
        i_cat = jnp.concatenate([i_hi, i_lo], axis=1)
        made[t] = lax.dot_general(v_cat, i_cat, NT, preferred_element_type=F32) + lax.dot_general(
            v_lo, i_hi, NT, preferred_element_type=F32
        )
        place = pl.ds(pl.multiple_of(r * points, points), points)

        def send_rows(i, carry):
            j = lax.rem(i + r, group)
            target = f * group + j
            src = made.at[t, pl.ds(pl.multiple_of(j * rows, rows), rows)]

            @pl.when(target != r)
            def _():
                pltpu.make_async_remote_copy(
                    src_ref=src,
                    dst_ref=out.at[:, place],
                    send_sem=send_sem,
                    recv_sem=recv_sem,
                    device_id=(b, target),
                    device_id_type=MESH,
                ).start()

            @pl.when(target == r)
            def _():
                pltpu.make_async_copy(src, out.at[:, place], own_sem).start()

            return carry

        lax.fori_loop(0, group, send_rows, 0)
        return carry

    lax.fori_loop(0, n_fields, one_field, 0)

    def halo_sent(t, carry):
        @pl.when(b < bands - 1)
        def _():
            halo_copy(t, 0, b, r).wait_send()

        @pl.when(b > 0)
        def _():
            halo_copy(t, 1, b, r).wait_send()

        halo_copy(t, 2, b, east).wait_send()
        halo_copy(t, 3, b, west).wait_send()
        return carry

    lax.fori_loop(0, n_fields, halo_sent, 0)
    mine = out.at[:, : points]
    pltpu.make_async_copy(mine, mine, own_sem).wait()
    others = out.at[:, : (regions - 1) * points]
    pltpu.make_async_copy(others, others, send_sem).wait()
    pltpu.make_async_copy(others, others, recv_sem).wait()


def solution(mesh):
    bands, regions = mesh.shape["band"], mesh.shape["region"]

    def body(fields, send_list, departure, hweight, base_level, vweight, vertical_op):
        points, width = fields.shape
        n_fields = width // LEV
        stencil = departure.shape[0]
        lists = send_list.transpose(0, 2, 3, 1).reshape(bands * 4, 2, regions)
        extended = points * 5
        anywhere = pl.BlockSpec(memory_space=pl.ANY)
        resident = anywhere
        return pl.pallas_call(
            functools.partial(kernel, bands, regions),
            out_shape=jax.ShapeDtypeStruct((width // regions, points * regions), F32),
            in_specs=[resident] * 7,
            out_specs=anywhere,
            scratch_shapes=[
                pltpu.VMEM((points, width), F32),
                pltpu.VMEM((n_fields, 4, points, LEV), F32),
                pltpu.SMEM(lists.shape, jnp.int32),
                pltpu.VMEM(departure.shape, jnp.int32),
                pltpu.VMEM(hweight.shape, F32),
                pltpu.VMEM(base_level.shape, jnp.int32),
                pltpu.VMEM(vweight.shape, F32),
                pltpu.VMEM(vertical_op.shape, F32),
                pltpu.VMEM((points, stencil), jnp.int32),
                pltpu.VMEM((points, stencil), F32),
                pltpu.VMEM((points, extended), F32),
                pltpu.VMEM((points, extended), BF16),
                pltpu.VMEM((points, extended), BF16),
                pltpu.VMEM((extended, 2 * LEV), BF16),
                pltpu.VMEM((points, LEV), jnp.int32),
                pltpu.VMEM((4, points, LEV), F32),
                pltpu.VMEM((n_fields, LEV, points), F32),
                pltpu.SemaphoreType.DMA((7,)),
                pltpu.SemaphoreType.DMA((n_fields, 4)),
                pltpu.SemaphoreType.DMA((n_fields, 4)),
                pltpu.SemaphoreType.DMA,
                pltpu.SemaphoreType.DMA,
                pltpu.SemaphoreType.DMA,
            ],
            compiler_params=pltpu.CompilerParams(
                collective_id=0, has_side_effects=True, vmem_limit_bytes=63 * 2**20
            ),
            name="semi_lagrangian",
        )(fields, lists, departure, hweight, base_level, vweight, vertical_op)

    points_last = P(None, ("band", "region"))
    return jax.shard_map(
        body,
        mesh=mesh,
        in_specs=(
            P(("band", "region"), None),
            P(),
            points_last,
            points_last,
            points_last,
            P(None, None, ("band", "region")),
            P(),
        ),
        out_specs=P("region", "band"),
        check_vma=False,
    )
```

```python
import functools

import jax
import jax.numpy as jnp
from jax import lax
from jax.experimental import pallas as pl
from jax.experimental.pallas import tpu as pltpu
from jax.sharding import PartitionSpec as P

MESH = pl.DeviceIdType.MESH
LEV = 128
LANES = 128
FAR = 1 << 20
F32, BF16 = jnp.float32, jnp.bfloat16
NT = (((1,), (1,)), ((), ()))


def halves(x):
    high = x.astype(BF16)
    return high, (x - high.astype(F32)).astype(BF16)


def kernel(
    bands, regions, fields, lists, departure, hweight, base_level, vweight, vertical_op, out,
    own, halo, lists_s, dep_v, hw_v, base_v, vw_v, vop_v, dep_t, hw_t, w_hi, w_lo, e_cat, base_t, vw_t, made, near_sum,
    in_sem, halo_send, halo_recv, own_sem, send_sem, recv_sem, plane_sem,
):
    b, r = lax.axis_index("band"), lax.axis_index("region")
    points = fields.shape[0]
    n_fields = fields.shape[1] // LEV
    group = regions // n_fields
    rows = LEV // group
    plane = min(8, regions // 2)
    planes = regions // plane
    z, spot = r // plane, lax.rem(r, plane)
    east, west = lax.rem(r + 1, regions), lax.rem(r + regions - 1, regions)

    def signal(sem, band, region):
        pl.semaphore_signal(sem, inc=1, device_id=(band, region), device_id_type=MESH)

    barrier = pltpu.get_barrier_semaphore()

    @pl.when(b > 0)
    def _():
        signal(barrier, b - 1, r)

    @pl.when(b < bands - 1)
    def _():
        signal(barrier, b + 1, r)

    @pl.when(spot == plane - 1)
    def _():
        signal(barrier, b, east)

    @pl.when(spot == 0)
    def _():
        signal(barrier, b, west)

    def plane_mate(i):
        return z * plane + lax.rem(spot + i, plane)

    for i in range(1, plane):
        signal(barrier, b, plane_mate(i))
    for i in range(1, planes):
        signal(barrier, b, lax.rem(r + i * plane, regions))

    loads = [
        pltpu.make_async_copy(src, dst, in_sem.at[i])
        for i, (src, dst) in enumerate(
            [(departure, dep_v), (hweight, hw_v), (lists, lists_s), (base_level, base_v), (vweight, vw_v), (vertical_op, vop_v), (fields, own)]
        )
    ]
    for load in loads:
        load.start()

    edges = jnp.minimum(b, 1) + jnp.minimum(bands - 1 - b, 1)
    corners = (1 - jnp.minimum(spot, 1)) + (1 - jnp.minimum(plane - 1 - spot, 1))
    pl.semaphore_wait(barrier, plane + planes - 2 + edges + corners)

    def offset(t):
        return lax.rem(2 + t * (t + 1) // 2, n_fields)

    def field_of(region, t):
        return lax.rem(region // group + offset(t), n_fields)

    def halo_copy(t, d, band, region):
        column = pl.multiple_of(field_of(region, t) * LEV, LEV)
        return pltpu.make_async_remote_copy(
            src_ref=fields.at[:, pl.ds(column, LEV)],
            dst_ref=halo.at[t, d],
            send_sem=halo_send.at[t, d],
            recv_sem=halo_recv.at[t, d],
            device_id=(band, region),
            device_id_type=MESH,
        )

    def send_halo(t, carry):
        @pl.when(b < bands - 1)
        def _():
            halo_copy(t, 0, b + 1, r).start()

        @pl.when(b > 0)
        def _():
            halo_copy(t, 1, b - 1, r).start()

        halo_copy(t, 2, b, east).start()
        halo_copy(t, 3, b, west).start()
        return carry

    lax.fori_loop(0, n_fields, send_halo, 0)
    for i in range(1, plane):
        signal(plane_sem, b, plane_mate(i))

    def blank(d):
        def one(t, carry):
            halo[t, d] = jnp.zeros(halo.shape[2:], F32)
            return carry

        lax.fori_loop(0, n_fields, one, 0)

    @pl.when(b == 0)
    def _():
        blank(0)

    @pl.when(b == bands - 1)
    def _():
        blank(1)

    for load in loads[:3]:
        load.wait()

    blocks = points // LANES
    bases = [i * LANES for i in range(blocks)]
    before, after = jnp.maximum(b - 1, 0), jnp.minimum(b + 1, bands - 1)
    for d, band, region in [(2, b, west), (3, b, east), (0, before, r), (1, after, r)]:
        first, second = (lists_s[band * 4 + d, e, region] for e in range(2))
        part = points + d * points
        for block in range(blocks):
            bases.append(jnp.where(first == block, part, jnp.where(second == block, part + LANES, FAR)))

    dep_t[...] = jnp.transpose(dep_v[...])
    hw_t[...] = jnp.transpose(hw_v[...])
    stencil = dep_v.shape[0]

    def weigh(i, carry):
        rows_i = pl.ds(pl.multiple_of(i * 16, 16), 16)
        dep, hw = dep_t[rows_i, :], hw_t[rows_i, :]
        lane = lax.broadcasted_iota(jnp.int32, (8, LANES), 1)
        sides = []
        for s in range(2):
            deps = [jnp.broadcast_to(dep[s * 8 : s * 8 + 8, c : c + 1], (8, LANES)) for c in range(stencil)]
            hws = [jnp.broadcast_to(hw[s * 8 : s * 8 + 8, c : c + 1], (8, LANES)) for c in range(stencil)]
            totals = []
            for base in bases:
                target = lane + base
                total = jnp.where(deps[0] == target, hws[0], 0.0)
                for c in range(1, stencil):
                    total = total + jnp.where(deps[c] == target, hws[c], 0.0)
                totals.append(total)
            sides.append(totals)
        for j in range(len(bases)):
            hi, lo = halves(jnp.concatenate([sides[0][j], sides[1][j]], axis=0))
            w_hi[rows_i, j * LANES : (j + 1) * LANES] = hi
            w_lo[rows_i, j * LANES : (j + 1) * LANES] = lo
        return carry

    lax.fori_loop(0, points // 16, weigh, 0, unroll=4)
    for load in loads[3:]:
        load.wait()
    base_t[...] = jnp.transpose(base_v[...])
    for m in range(4):
        vw_t[m] = jnp.transpose(vw_v[m])
    v_hi, v_lo = halves(vop_v[...])
    v_cat = jnp.concatenate([v_hi, v_hi], axis=1)

    def product(first, last):
        both = jnp.dot(w_hi[:, first:last], e_cat[first:last, :], preferred_element_type=F32)
        rest = jnp.dot(w_lo[:, first:last], e_cat[first:last, :LEV], preferred_element_type=F32)
        return both[:, :LEV] + both[:, LEV:] + rest

    def one_field(t, carry):
        f = field_of(r, t)
        column = pl.multiple_of(f * LEV, LEV)
        near = 3 * points
        e_cat[:points, :LEV], e_cat[:points, LEV:] = halves(own[:, pl.ds(column, LEV)])
        for d in (2, 3):
            halo_copy(t, d, b, r).wait_recv()
            part = slice((d - 1) * points, d * points)
            e_cat[part, :LEV], e_cat[part, LEV:] = halves(halo[t, d])
        near_sum[...] = product(0, near)

        @pl.when(b > 0)
        def _():
            halo_copy(t, 0, b, r).wait_recv()

        @pl.when(b < bands - 1)
        def _():
            halo_copy(t, 1, b, r).wait_recv()

        for d in (0, 1):
            part = slice((d + 3) * points, (d + 4) * points)
            e_cat[part, :LEV], e_cat[part, LEV:] = halves(halo[t, d])
        horizontal = near_sum[...] + product(near, 5 * points)
        mixed = jnp.zeros((points, LEV), F32)
        for m in range(4):
            picked = jnp.take_along_axis(horizontal, base_t[...] + (m - 1), axis=1, mode="promise_in_bounds")
            mixed = mixed + vw_t[m] * picked
        i_hi, i_lo = halves(mixed)
        i_cat = jnp.concatenate([i_hi, i_lo], axis=1)
        made[t] = lax.dot_general(v_cat, i_cat, NT, preferred_element_type=F32) + lax.dot_general(
            v_lo, i_hi, NT, preferred_element_type=F32
        )

        @pl.when(t == 0)
        def _():
            pl.semaphore_wait(plane_sem, plane - 1)

        place = pl.ds(pl.multiple_of(r * points, points), points)

        def send_rows(i, carry):
            j = lax.rem(i + r, group)
            target = f * group + j
            src = made.at[t, pl.ds(pl.multiple_of(j * rows, rows), rows)]
            dst = out.at[:, place]

            @pl.when(target != r)
            def _():
                pltpu.make_async_remote_copy(
                    src_ref=src,
                    dst_ref=dst,
                    send_sem=send_sem,
                    recv_sem=recv_sem,
                    device_id=(b, target),
                    device_id_type=MESH,
                ).start()

            @pl.when(target == r)
            def _():
                pltpu.make_async_copy(src, dst, own_sem).start()

            return carry

        lax.fori_loop(0, group, send_rows, 0)
        return carry

    lax.fori_loop(0, n_fields, one_field, 0)

    def halo_sent(t, carry):
        @pl.when(b < bands - 1)
        def _():
            halo_copy(t, 0, b, r).wait_send()

        @pl.when(b > 0)
        def _():
            halo_copy(t, 1, b, r).wait_send()

        halo_copy(t, 2, b, east).wait_send()
        halo_copy(t, 3, b, west).wait_send()
        return carry

    lax.fori_loop(0, n_fields, halo_sent, 0)
    mine = out.at[:, :points]
    pltpu.make_async_copy(mine, mine, own_sem).wait()
    others = out.at[:, : (regions - 1) * points]
    pltpu.make_async_copy(others, others, send_sem).wait()
    pltpu.make_async_copy(others, others, recv_sem).wait()


def solution(mesh):
    bands, regions = mesh.shape["band"], mesh.shape["region"]

    def body(fields, send_list, departure, hweight, base_level, vweight, vertical_op):
        points, width = fields.shape
        n_fields = width // LEV
        stencil = departure.shape[0]
        lists = send_list.transpose(0, 2, 3, 1).reshape(bands * 4, 2, regions)
        extended = points * 5
        anywhere = pl.BlockSpec(memory_space=pl.ANY)
        rows = width // regions
        return pl.pallas_call(
            functools.partial(kernel, bands, regions),
            out_shape=pltpu.VMEM((rows, points * regions), F32),
            in_specs=[anywhere] * 7,
            out_specs=anywhere,
            scratch_shapes=[
                pltpu.VMEM((points, width), F32),
                pltpu.VMEM((n_fields, 4, points, LEV), F32),
                pltpu.SMEM(lists.shape, jnp.int32),
                pltpu.VMEM(departure.shape, jnp.int32),
                pltpu.VMEM(hweight.shape, F32),
                pltpu.VMEM(base_level.shape, jnp.int32),
                pltpu.VMEM(vweight.shape, F32),
                pltpu.VMEM(vertical_op.shape, F32),
                pltpu.VMEM((points, stencil), jnp.int32),
                pltpu.VMEM((points, stencil), F32),
                pltpu.VMEM((points, extended), BF16),
                pltpu.VMEM((points, extended), BF16),
                pltpu.VMEM((extended, 2 * LEV), BF16),
                pltpu.VMEM((points, LEV), jnp.int32),
                pltpu.VMEM((4, points, LEV), F32),
                pltpu.VMEM((n_fields, LEV, points), F32),
                pltpu.VMEM((points, LEV), F32),
                pltpu.SemaphoreType.DMA((7,)),
                pltpu.SemaphoreType.DMA((n_fields, 4)),
                pltpu.SemaphoreType.DMA((n_fields, 4)),
                pltpu.SemaphoreType.DMA,
                pltpu.SemaphoreType.DMA,
                pltpu.SemaphoreType.DMA,
                pltpu.SemaphoreType.REGULAR,
            ],
            compiler_params=pltpu.CompilerParams(
                collective_id=0, has_side_effects=True, vmem_limit_bytes=32 * 2**20
            ),
            name="semi_lagrangian",
        )(*[pltpu.with_memory_space_constraint(a, pltpu.HBM) for a in (fields, lists, departure, hweight, base_level, vweight, vertical_op)])

    points_last = P(None, ("band", "region"))
    return jax.shard_map(
        body,
        mesh=mesh,
        in_specs=(
            P(("band", "region"), None),
            P(),
            points_last,
            points_last,
            points_last,
            P(None, None, ("band", "region")),
            P(),
        ),
        out_specs=P("region", "band"),
        check_vma=False,
    )
```

```python
import functools

import jax
import jax.numpy as jnp
from jax import lax
from jax.experimental import pallas as pl
from jax.experimental.pallas import tpu as pltpu
from jax.sharding import PartitionSpec as P

MESH = pl.DeviceIdType.MESH
LEV = 128
LANES = 128
FAR = 1 << 20
F32, BF16 = jnp.float32, jnp.bfloat16
NT = (((1,), (1,)), ((), ()))


def halves(x):
    high = x.astype(BF16)
    return high, (x - high.astype(F32)).astype(BF16)


def kernel(
    bands, regions, fields, lists, departure, hweight, base_level, vweight, vertical_op, out,
    own, halo, lists_s, dep_v, hw_v, base_v, vw_v, vop_v, dep_t, hw_t, w_hi, w_lo, e_cat, base_t, vw_t, made, near_sum,
    in_sem, halo_send, halo_recv, own_sem, send_sem, recv_sem, plane_sem, gate_sem,
):
    b, r = lax.axis_index("band"), lax.axis_index("region")
    points = fields.shape[0]
    n_fields = fields.shape[1] // LEV
    group = regions // n_fields
    rows = LEV // group
    plane = min(8, regions // 2)
    planes = regions // plane
    z, spot = r // plane, lax.rem(r, plane)
    gate = plane // 2
    east, west = lax.rem(r + 1, regions), lax.rem(r + regions - 1, regions)

    def signal(sem, band, region):
        pl.semaphore_signal(sem, inc=1, device_id=(band, region), device_id_type=MESH)

    barrier = pltpu.get_barrier_semaphore()

    @pl.when(b > 0)
    def _():
        signal(barrier, b - 1, r)

    @pl.when(b < bands - 1)
    def _():
        signal(barrier, b + 1, r)

    @pl.when(spot == plane - 1)
    def _():
        signal(barrier, b, east)

    @pl.when(spot == 0)
    def _():
        signal(barrier, b, west)

    def plane_mate(i):
        return z * plane + lax.rem(spot + i, plane)

    for i in range(1, plane):
        signal(barrier, b, plane_mate(i))

    @pl.when(spot == gate)
    def _():
        for i in range(1, planes):
            signal(barrier, b, lax.rem(r + i * plane, regions))

    loads = [
        pltpu.make_async_copy(src, dst, in_sem.at[i])
        for i, (src, dst) in enumerate(
            [(departure, dep_v), (hweight, hw_v), (lists, lists_s), (base_level, base_v), (vweight, vw_v), (vertical_op, vop_v), (fields, own)]
        )
    ]
    for load in loads:
        load.start()

    edges = jnp.minimum(b, 1) + jnp.minimum(bands - 1 - b, 1)
    corners = (1 - jnp.minimum(spot, 1)) + (1 - jnp.minimum(plane - 1 - spot, 1))
    at_gate = jnp.where(spot == gate, 1, 0)
    pl.semaphore_wait(barrier, plane - 1 + at_gate * (planes - 1) + edges + corners)

    def field_of(region, t):
        pair = region // group
        return 2 * lax.rem(pair // 2 + 1 + t // 2, 2) + lax.rem(pair + t + t // 2, 2)

    def halo_copy(t, d, band, region):
        column = pl.multiple_of(field_of(region, t) * LEV, LEV)
        return pltpu.make_async_remote_copy(
            src_ref=fields.at[:, pl.ds(column, LEV)],
            dst_ref=halo.at[t, d],
            send_sem=halo_send.at[t, d],
            recv_sem=halo_recv.at[t, d],
            device_id=(band, region),
            device_id_type=MESH,
        )

    def send_halo(t, carry):
        @pl.when(b < bands - 1)
        def _():
            halo_copy(t, 0, b + 1, r).start()

        @pl.when(b > 0)
        def _():
            halo_copy(t, 1, b - 1, r).start()

        halo_copy(t, 2, b, east).start()
        halo_copy(t, 3, b, west).start()
        return carry

    lax.fori_loop(0, n_fields, send_halo, 0)

    @pl.when(spot == gate)
    def _():
        for i in range(1, planes):
            signal(gate_sem, b, lax.rem(r + i * plane, regions))
        pl.semaphore_wait(gate_sem, planes - 1)
        for i in range(1, plane):
            signal(plane_sem, b, plane_mate(i))

    def blank(d):
        def one(t, carry):
            halo[t, d] = jnp.zeros(halo.shape[2:], F32)
            return carry

        lax.fori_loop(0, n_fields, one, 0)

    @pl.when(b == 0)
    def _():
        blank(0)

    @pl.when(b == bands - 1)
    def _():
        blank(1)

    for load in loads[:3]:
        load.wait()

    blocks = points // LANES
    bases = [i * LANES for i in range(blocks)]
    before, after = jnp.maximum(b - 1, 0), jnp.minimum(b + 1, bands - 1)
    for d, band, region in [(2, b, west), (3, b, east), (0, before, r), (1, after, r)]:
        first, second = (lists_s[band * 4 + d, e, region] for e in range(2))
        part = points + d * points
        for block in range(blocks):
            bases.append(jnp.where(first == block, part, jnp.where(second == block, part + LANES, FAR)))

    dep_t[...] = jnp.transpose(dep_v[...])
    hw_t[...] = jnp.transpose(hw_v[...])
    stencil = dep_v.shape[0]

    def weigh(i, carry):
        rows_i = pl.ds(pl.multiple_of(i * 16, 16), 16)
        dep, hw = dep_t[rows_i, :], hw_t[rows_i, :]
        lane = lax.broadcasted_iota(jnp.int32, (8, LANES), 1)
        sides = []
        for s in range(2):
            deps = [jnp.broadcast_to(dep[s * 8 : s * 8 + 8, c : c + 1], (8, LANES)) for c in range(stencil)]
            hws = [jnp.broadcast_to(hw[s * 8 : s * 8 + 8, c : c + 1], (8, LANES)) for c in range(stencil)]
            totals = []
            for base in bases:
                target = lane + base
                total = jnp.where(deps[0] == target, hws[0], 0.0)
                for c in range(1, stencil):
                    total = total + jnp.where(deps[c] == target, hws[c], 0.0)
                totals.append(total)
            sides.append(totals)
        for j in range(len(bases)):
            hi, lo = halves(jnp.concatenate([sides[0][j], sides[1][j]], axis=0))
            w_hi[rows_i, j * LANES : (j + 1) * LANES] = hi
            w_lo[rows_i, j * LANES : (j + 1) * LANES] = lo
        return carry

    lax.fori_loop(0, points // 16, weigh, 0, unroll=4)
    for load in loads[3:]:
        load.wait()
    base_t[...] = jnp.transpose(base_v[...])
    for m in range(4):
        vw_t[m] = jnp.transpose(vw_v[m])
    v_hi, v_lo = halves(vop_v[...])
    v_cat = jnp.concatenate([v_hi, v_hi], axis=1)

    def product(first, last):
        both = jnp.dot(w_hi[:, first:last], e_cat[first:last, :], preferred_element_type=F32)
        rest = jnp.dot(w_lo[:, first:last], e_cat[first:last, :LEV], preferred_element_type=F32)
        return both[:, :LEV] + both[:, LEV:] + rest

    def one_field(t, carry):
        f = field_of(r, t)
        column = pl.multiple_of(f * LEV, LEV)
        near = 3 * points
        e_cat[:points, :LEV], e_cat[:points, LEV:] = halves(own[:, pl.ds(column, LEV)])
        for d in (2, 3):
            halo_copy(t, d, b, r).wait_recv()
            part = slice((d - 1) * points, d * points)
            e_cat[part, :LEV], e_cat[part, LEV:] = halves(halo[t, d])
        near_sum[...] = product(0, near)

        @pl.when(b > 0)
        def _():
            halo_copy(t, 0, b, r).wait_recv()

        @pl.when(b < bands - 1)
        def _():
            halo_copy(t, 1, b, r).wait_recv()

        for d in (0, 1):
            part = slice((d + 3) * points, (d + 4) * points)
            e_cat[part, :LEV], e_cat[part, LEV:] = halves(halo[t, d])
        horizontal = near_sum[...] + product(near, 5 * points)
        mixed = jnp.zeros((points, LEV), F32)
        for m in range(4):
            picked = jnp.take_along_axis(horizontal, base_t[...] + (m - 1), axis=1, mode="promise_in_bounds")
            mixed = mixed + vw_t[m] * picked
        i_hi, i_lo = halves(mixed)
        i_cat = jnp.concatenate([i_hi, i_lo], axis=1)
        made[t] = lax.dot_general(v_cat, i_cat, NT, preferred_element_type=F32) + lax.dot_general(
            v_lo, i_hi, NT, preferred_element_type=F32
        )

        @pl.when((t == 0) & (spot != gate))
        def _():
            pl.semaphore_wait(plane_sem, 1)

        place = pl.ds(pl.multiple_of(r * points, points), points)

        def send_rows(i, carry):
            target = f * group + i
            src = made.at[t, pl.ds(pl.multiple_of(i * rows, rows), rows)]
            dst = out.at[:, place]

            @pl.when(target != r)
            def _():
                pltpu.make_async_remote_copy(
                    src_ref=src,
                    dst_ref=dst,
                    send_sem=send_sem,
                    recv_sem=recv_sem,
                    device_id=(b, target),
                    device_id_type=MESH,
                ).start()

            @pl.when(target == r)
            def _():
                pltpu.make_async_copy(src, dst, own_sem).start()

            return carry

        lax.fori_loop(0, group, send_rows, 0)
        return carry

    lax.fori_loop(0, n_fields, one_field, 0)

    def halo_sent(t, carry):
        @pl.when(b < bands - 1)
        def _():
            halo_copy(t, 0, b, r).wait_send()

        @pl.when(b > 0)
        def _():
            halo_copy(t, 1, b, r).wait_send()

        halo_copy(t, 2, b, east).wait_send()
        halo_copy(t, 3, b, west).wait_send()
        return carry

    lax.fori_loop(0, n_fields, halo_sent, 0)
    mine = out.at[:, :points]
    pltpu.make_async_copy(mine, mine, own_sem).wait()
    others = out.at[:, : (regions - 1) * points]
    pltpu.make_async_copy(others, others, send_sem).wait()
    pltpu.make_async_copy(others, others, recv_sem).wait()


def solution(mesh):
    bands, regions = mesh.shape["band"], mesh.shape["region"]

    def body(fields, send_list, departure, hweight, base_level, vweight, vertical_op):
        points, width = fields.shape
        n_fields = width // LEV
        stencil = departure.shape[0]
        lists = send_list.transpose(0, 2, 3, 1).reshape(bands * 4, 2, regions)
        extended = points * 5
        anywhere = pl.BlockSpec(memory_space=pl.ANY)
        rows = width // regions
        return pl.pallas_call(
            functools.partial(kernel, bands, regions),
            out_shape=pltpu.VMEM((rows, points * regions), F32),
            in_specs=[anywhere] * 7,
            out_specs=anywhere,
            scratch_shapes=[
                pltpu.VMEM((points, width), F32),
                pltpu.VMEM((n_fields, 4, points, LEV), F32),
                pltpu.SMEM(lists.shape, jnp.int32),
                pltpu.VMEM(departure.shape, jnp.int32),
                pltpu.VMEM(hweight.shape, F32),
                pltpu.VMEM(base_level.shape, jnp.int32),
                pltpu.VMEM(vweight.shape, F32),
                pltpu.VMEM(vertical_op.shape, F32),
                pltpu.VMEM((points, stencil), jnp.int32),
                pltpu.VMEM((points, stencil), F32),
                pltpu.VMEM((points, extended), BF16),
                pltpu.VMEM((points, extended), BF16),
                pltpu.VMEM((extended, 2 * LEV), BF16),
                pltpu.VMEM((points, LEV), jnp.int32),
                pltpu.VMEM((4, points, LEV), F32),
                pltpu.VMEM((n_fields, LEV, points), F32),
                pltpu.VMEM((points, LEV), F32),
                pltpu.SemaphoreType.DMA((7,)),
                pltpu.SemaphoreType.DMA((n_fields, 4)),
                pltpu.SemaphoreType.DMA((n_fields, 4)),
                pltpu.SemaphoreType.DMA,
                pltpu.SemaphoreType.DMA,
                pltpu.SemaphoreType.DMA,
                pltpu.SemaphoreType.REGULAR,
                pltpu.SemaphoreType.REGULAR,
            ],
            compiler_params=pltpu.CompilerParams(
                collective_id=0, has_side_effects=True, vmem_limit_bytes=32 * 2**20
            ),
            name="semi_lagrangian",
        )(*[pltpu.with_memory_space_constraint(a, pltpu.HBM) for a in (fields, lists, departure, hweight, base_level, vweight, vertical_op)])

    points_last = P(None, ("band", "region"))
    return jax.shard_map(
        body,
        mesh=mesh,
        in_specs=(
            P(("band", "region"), None),
            P(),
            points_last,
            points_last,
            points_last,
            P(None, None, ("band", "region")),
            P(),
        ),
        out_specs=P("region", "band"),
        check_vma=False,
    )
```

```python
import functools

import jax
import jax.numpy as jnp
from jax import lax
from jax.experimental import pallas as pl
from jax.experimental.pallas import tpu as pltpu
from jax.sharding import PartitionSpec as P

MESH = pl.DeviceIdType.MESH
LEV = 128
LANES = 128
FAR = 1 << 20
F32, BF16 = jnp.float32, jnp.bfloat16
NT = (((1,), (1,)), ((), ()))


def halves(x):
    high = x.astype(BF16)
    return high, (x - high.astype(F32)).astype(BF16)


def kernel(
    bands, regions, fields, lists, departure, hweight, base_level, vweight, vertical_op, out,
    own, halo, lists_s, dep_v, hw_v, base_v, vw_v, vop_v, dep_t, hw_t, w_hi, w_lo, e_cat, base_t, vw_t, made, near_sum,
    in_sem, halo_send, halo_recv, own_sem, send_sem, recv_sem, plane_sem, gate_sem,
):
    b, r = lax.axis_index("band"), lax.axis_index("region")
    points = fields.shape[0]
    n_fields = fields.shape[1] // LEV
    group = regions // n_fields
    rows = LEV // group
    plane = min(8, regions // 2)
    planes = regions // plane
    z, spot = r // plane, lax.rem(r, plane)
    gate = plane // 2
    east, west = lax.rem(r + 1, regions), lax.rem(r + regions - 1, regions)

    def signal(sem, band, region):
        pl.semaphore_signal(sem, inc=1, device_id=(band, region), device_id_type=MESH)

    barrier = pltpu.get_barrier_semaphore()

    @pl.when(b > 0)
    def _():
        signal(barrier, b - 1, r)

    @pl.when(b < bands - 1)
    def _():
        signal(barrier, b + 1, r)

    @pl.when(spot == plane - 1)
    def _():
        signal(barrier, b, east)

    @pl.when(spot == 0)
    def _():
        signal(barrier, b, west)

    def plane_mate(i):
        return z * plane + lax.rem(spot + i, plane)

    for i in range(1, plane):
        signal(barrier, b, plane_mate(i))

    @pl.when(spot == gate)
    def _():
        for i in range(1, planes):
            signal(barrier, b, lax.rem(r + i * plane, regions))

    loads = [
        pltpu.make_async_copy(src, dst, in_sem.at[i])
        for i, (src, dst) in enumerate(
            [(departure, dep_v), (hweight, hw_v), (lists, lists_s), (base_level, base_v), (vweight, vw_v), (vertical_op, vop_v), (fields, own)]
        )
    ]
    for load in loads:
        load.start()

    def blank(d):
        def one(t, carry):
            halo[t, d] = jnp.zeros(halo.shape[2:], F32)
            return carry

        lax.fori_loop(0, n_fields, one, 0)

    @pl.when(b == 0)
    def _():
        blank(0)

    @pl.when(b == bands - 1)
    def _():
        blank(1)

    edges = jnp.minimum(b, 1) + jnp.minimum(bands - 1 - b, 1)
    corners = (1 - jnp.minimum(spot, 1)) + (1 - jnp.minimum(plane - 1 - spot, 1))
    at_gate = jnp.where(spot == gate, 1, 0)
    pl.semaphore_wait(barrier, plane - 1 + at_gate * (planes - 1) + edges + corners)

    def field_of(region, t):
        pair = region // group
        flip = (pair // 3) * (1 - t // 2)
        return 2 * lax.rem(pair // 2 + 1 + t // 2, 2) + lax.rem(pair + t + t // 2 + flip, 2)

    def halo_copy(t, d, band, region):
        column = pl.multiple_of(field_of(region, t) * LEV, LEV)
        return pltpu.make_async_remote_copy(
            src_ref=fields.at[:, pl.ds(column, LEV)],
            dst_ref=halo.at[t, d],
            send_sem=halo_send.at[t, d],
            recv_sem=halo_recv.at[t, d],
            device_id=(band, region),
            device_id_type=MESH,
        )

    def send_halo(t, carry):
        @pl.when(b < bands - 1)
        def _():
            halo_copy(t, 0, b + 1, r).start()

        @pl.when(b > 0)
        def _():
            halo_copy(t, 1, b - 1, r).start()

        halo_copy(t, 2, b, east).start()
        halo_copy(t, 3, b, west).start()
        return carry

    @pl.when(spot == gate)
    def _():
        for i in range(1, planes):
            signal(gate_sem, b, lax.rem(r + i * plane, regions))

    lax.fori_loop(0, n_fields, send_halo, 0)


    for load in loads[:3]:
        load.wait()

    blocks = points // LANES
    bases = [i * LANES for i in range(blocks)]
    before, after = jnp.maximum(b - 1, 0), jnp.minimum(b + 1, bands - 1)
    for d, band, region in [(2, b, west), (3, b, east), (0, before, r), (1, after, r)]:
        first, second = (lists_s[band * 4 + d, e, region] for e in range(2))
        part = points + d * points
        for block in range(blocks):
            bases.append(jnp.where(first == block, part, jnp.where(second == block, part + LANES, FAR)))

    dep_t[...] = jnp.transpose(dep_v[...])
    hw_t[...] = jnp.transpose(hw_v[...])
    stencil = dep_v.shape[0]

    def weigh(i, carry):
        rows_i = pl.ds(pl.multiple_of(i * 16, 16), 16)
        dep, hw = dep_t[rows_i, :], hw_t[rows_i, :]
        lane = lax.broadcasted_iota(jnp.int32, (8, LANES), 1)
        sides = []
        for s in range(2):
            deps = [jnp.broadcast_to(dep[s * 8 : s * 8 + 8, c : c + 1], (8, LANES)) for c in range(stencil)]
            hws = [jnp.broadcast_to(hw[s * 8 : s * 8 + 8, c : c + 1], (8, LANES)) for c in range(stencil)]
            totals = []
            for base in bases:
                target = lane + base
                total = jnp.where(deps[0] == target, hws[0], 0.0)
                for c in range(1, stencil):
                    total = total + jnp.where(deps[c] == target, hws[c], 0.0)
                totals.append(total)
            sides.append(totals)
        for j in range(len(bases)):
            hi, lo = halves(jnp.concatenate([sides[0][j], sides[1][j]], axis=0))
            w_hi[rows_i, j * LANES : (j + 1) * LANES] = hi
            w_lo[rows_i, j * LANES : (j + 1) * LANES] = lo
        return carry

    lax.fori_loop(0, points // 16, weigh, 0, unroll=4)

    @pl.when(spot == gate)
    def _():
        pl.semaphore_wait(gate_sem, planes - 1)
        for i in range(1, plane):
            signal(plane_sem, b, plane_mate(i))

    for load in loads[3:]:
        load.wait()
    base_t[...] = jnp.transpose(base_v[...])
    for m in range(4):
        vw_t[m] = jnp.transpose(vw_v[m])
    v_hi, v_lo = halves(vop_v[...])
    v_cat = jnp.concatenate([v_hi, v_hi], axis=1)

    def product(first, last):
        both = jnp.dot(w_hi[:, first:last], e_cat[first:last, :], preferred_element_type=F32)
        rest = jnp.dot(w_lo[:, first:last], e_cat[first:last, :LEV], preferred_element_type=F32)
        return both[:, :LEV] + both[:, LEV:] + rest

    def one_field(t, carry):
        f = field_of(r, t)
        column = pl.multiple_of(f * LEV, LEV)
        near = 3 * points
        e_cat[:points, :LEV], e_cat[:points, LEV:] = halves(own[:, pl.ds(column, LEV)])
        for d in (2, 3):
            halo_copy(t, d, b, r).wait_recv()
            part = slice((d - 1) * points, d * points)
            e_cat[part, :LEV], e_cat[part, LEV:] = halves(halo[t, d])
        near_sum[...] = product(0, near)

        @pl.when(b > 0)
        def _():
            halo_copy(t, 0, b, r).wait_recv()

        @pl.when(b < bands - 1)
        def _():
            halo_copy(t, 1, b, r).wait_recv()

        for d in (0, 1):
            part = slice((d + 3) * points, (d + 4) * points)
            e_cat[part, :LEV], e_cat[part, LEV:] = halves(halo[t, d])
        horizontal = near_sum[...] + product(near, 5 * points)
        mixed = jnp.zeros((points, LEV), F32)
        for m in range(4):
            picked = jnp.take_along_axis(horizontal, base_t[...] + (m - 1), axis=1, mode="promise_in_bounds")
            mixed = mixed + vw_t[m] * picked
        i_hi, i_lo = halves(mixed)
        i_cat = jnp.concatenate([i_hi, i_lo], axis=1)
        made[t] = lax.dot_general(v_cat, i_cat, NT, preferred_element_type=F32) + lax.dot_general(
            v_lo, i_hi, NT, preferred_element_type=F32
        )

        @pl.when((t == 0) & (spot != gate))
        def _():
            pl.semaphore_wait(plane_sem, 1)

        place = pl.ds(pl.multiple_of(r * points, points), points)

        def send_rows(step, carry):
            i = step // 2 + lax.rem(step, 2) * (group // 2)
            target = f * group + i
            src = made.at[t, pl.ds(pl.multiple_of(i * rows, rows), rows)]
            dst = out.at[:, place]

            @pl.when(target != r)
            def _():
                pltpu.make_async_remote_copy(
                    src_ref=src,
                    dst_ref=dst,
                    send_sem=send_sem,
                    recv_sem=recv_sem,
                    device_id=(b, target),
                    device_id_type=MESH,
                ).start()

            @pl.when(target == r)
            def _():
                pltpu.make_async_copy(src, dst, own_sem).start()

            return carry

        lax.fori_loop(0, group, send_rows, 0)
        return carry

    lax.fori_loop(0, n_fields, one_field, 0)

    def halo_sent(t, carry):
        @pl.when(b < bands - 1)
        def _():
            halo_copy(t, 0, b, r).wait_send()

        @pl.when(b > 0)
        def _():
            halo_copy(t, 1, b, r).wait_send()

        halo_copy(t, 2, b, east).wait_send()
        halo_copy(t, 3, b, west).wait_send()
        return carry

    lax.fori_loop(0, n_fields, halo_sent, 0)
    mine = out.at[:, :points]
    pltpu.make_async_copy(mine, mine, own_sem).wait()
    others = out.at[:, : (regions - 1) * points]
    pltpu.make_async_copy(others, others, send_sem).wait()
    pltpu.make_async_copy(others, others, recv_sem).wait()


def solution(mesh):
    bands, regions = mesh.shape["band"], mesh.shape["region"]

    def body(fields, send_list, departure, hweight, base_level, vweight, vertical_op):
        points, width = fields.shape
        n_fields = width // LEV
        stencil = departure.shape[0]
        lists = send_list.transpose(0, 2, 3, 1).reshape(bands * 4, 2, regions)
        extended = points * 5
        anywhere = pl.BlockSpec(memory_space=pl.ANY)
        rows = width // regions
        return pl.pallas_call(
            functools.partial(kernel, bands, regions),
            out_shape=pltpu.VMEM((rows, points * regions), F32),
            in_specs=[anywhere] * 7,
            out_specs=anywhere,
            scratch_shapes=[
                pltpu.VMEM((points, width), F32),
                pltpu.VMEM((n_fields, 4, points, LEV), F32),
                pltpu.SMEM(lists.shape, jnp.int32),
                pltpu.VMEM(departure.shape, jnp.int32),
                pltpu.VMEM(hweight.shape, F32),
                pltpu.VMEM(base_level.shape, jnp.int32),
                pltpu.VMEM(vweight.shape, F32),
                pltpu.VMEM(vertical_op.shape, F32),
                pltpu.VMEM((points, stencil), jnp.int32),
                pltpu.VMEM((points, stencil), F32),
                pltpu.VMEM((points, extended), BF16),
                pltpu.VMEM((points, extended), BF16),
                pltpu.VMEM((extended, 2 * LEV), BF16),
                pltpu.VMEM((points, LEV), jnp.int32),
                pltpu.VMEM((4, points, LEV), F32),
                pltpu.VMEM((n_fields, LEV, points), F32),
                pltpu.VMEM((points, LEV), F32),
                pltpu.SemaphoreType.DMA((7,)),
                pltpu.SemaphoreType.DMA((n_fields, 4)),
                pltpu.SemaphoreType.DMA((n_fields, 4)),
                pltpu.SemaphoreType.DMA,
                pltpu.SemaphoreType.DMA,
                pltpu.SemaphoreType.DMA,
                pltpu.SemaphoreType.REGULAR,
                pltpu.SemaphoreType.REGULAR,
            ],
            compiler_params=pltpu.CompilerParams(
                collective_id=0, has_side_effects=True, vmem_limit_bytes=32 * 2**20
            ),
            name="semi_lagrangian",
        )(*[pltpu.with_memory_space_constraint(a, pltpu.HBM) for a in (fields, lists, departure, hweight, base_level, vweight, vertical_op)])

    points_last = P(None, ("band", "region"))
    return jax.shard_map(
        body,
        mesh=mesh,
        in_specs=(
            P(("band", "region"), None),
            P(),
            points_last,
            points_last,
            points_last,
            P(None, None, ("band", "region")),
            P(),
        ),
        out_specs=P("region", "band"),
        check_vma=False,
    )
```

```python
import functools

import jax
import jax.numpy as jnp
from jax import lax
from jax.experimental import pallas as pl
from jax.experimental.pallas import tpu as pltpu
from jax.sharding import PartitionSpec as P

MESH = pl.DeviceIdType.MESH
LEV = 128
LANES = 128
FAR = 1 << 20
F32, BF16 = jnp.float32, jnp.bfloat16
NT = (((1,), (1,)), ((), ()))


def halves(x):
    high = x.astype(BF16)
    return high, (x - high.astype(F32)).astype(BF16)


def kernel(
    bands, regions, fields, lists, departure, hweight, base_level, vweight, vertical_op, out,
    own, halo, lists_s, dep_v, hw_v, base_v, vw_v, vop_v, dep_t, hw_t, w_hi, w_lo, e_cat, base_t, vw_t, made, near_sum,
    in_sem, halo_send, halo_recv, own_sem, send_sem, recv_sem, plane_sem, gate_sem,
):
    b, r = lax.axis_index("band"), lax.axis_index("region")
    points = fields.shape[0]
    n_fields = fields.shape[1] // LEV
    group = regions // n_fields
    rows = LEV // group
    plane = min(8, regions // 2)
    planes = regions // plane
    z, spot = r // plane, lax.rem(r, plane)
    gate = plane // 2
    east, west = lax.rem(r + 1, regions), lax.rem(r + regions - 1, regions)

    def signal(sem, band, region):
        pl.semaphore_signal(sem, inc=1, device_id=(band, region), device_id_type=MESH)

    barrier = pltpu.get_barrier_semaphore()

    @pl.when(b > 0)
    def _():
        signal(barrier, b - 1, r)

    @pl.when(b < bands - 1)
    def _():
        signal(barrier, b + 1, r)

    @pl.when(spot == plane - 1)
    def _():
        signal(barrier, b, east)

    @pl.when(spot == 0)
    def _():
        signal(barrier, b, west)

    def plane_mate(i):
        return z * plane + lax.rem(spot + i, plane)

    for i in range(1, plane):
        signal(barrier, b, plane_mate(i))

    @pl.when(spot == gate)
    def _():
        for i in range(1, planes):
            signal(barrier, b, lax.rem(r + i * plane, regions))

    loads = [
        pltpu.make_async_copy(src, dst, in_sem.at[i])
        for i, (src, dst) in enumerate(
            [(departure, dep_v), (hweight, hw_v), (lists, lists_s), (base_level, base_v), (vweight, vw_v), (vertical_op, vop_v), (fields, own)]
        )
    ]
    for load in loads:
        load.start()

    def blank(d):
        def one(t, carry):
            halo[t, d] = jnp.zeros(halo.shape[2:], F32)
            return carry

        lax.fori_loop(0, n_fields, one, 0)

    @pl.when(b == 0)
    def _():
        blank(0)

    @pl.when(b == bands - 1)
    def _():
        blank(1)

    edges = jnp.minimum(b, 1) + jnp.minimum(bands - 1 - b, 1)
    corners = (1 - jnp.minimum(spot, 1)) + (1 - jnp.minimum(plane - 1 - spot, 1))
    at_gate = jnp.where(spot == gate, 1, 0)
    pl.semaphore_wait(barrier, plane - 1 + at_gate * (planes - 1) + edges + corners)

    def field_of(region, t):
        pair = region // group
        flip = (pair // 3) * (1 - t // 2)
        return 2 * lax.rem(pair // 2 + 1 + t // 2, 2) + lax.rem(pair + t + t // 2 + flip, 2)

    def halo_copy(t, d, band, region):
        column = pl.multiple_of(field_of(region, t) * LEV, LEV)
        return pltpu.make_async_remote_copy(
            src_ref=fields.at[:, pl.ds(column, LEV)],
            dst_ref=halo.at[t, d],
            send_sem=halo_send.at[t, d],
            recv_sem=halo_recv.at[t, d],
            device_id=(band, region),
            device_id_type=MESH,
        )

    def send_halo(t, carry):
        @pl.when(b < bands - 1)
        def _():
            halo_copy(t, 0, b + 1, r).start()

        @pl.when(b > 0)
        def _():
            halo_copy(t, 1, b - 1, r).start()

        halo_copy(t, 2, b, east).start()
        halo_copy(t, 3, b, west).start()
        return carry

    @pl.when(spot == gate)
    def _():
        for i in range(1, planes):
            signal(gate_sem, b, lax.rem(r + i * plane, regions))

    lax.fori_loop(0, n_fields, send_halo, 0)


    for load in loads[:3]:
        load.wait()

    blocks = points // LANES
    bases = [i * LANES for i in range(blocks)]
    before, after = jnp.maximum(b - 1, 0), jnp.minimum(b + 1, bands - 1)
    for d, band, region in [(2, b, west), (3, b, east), (0, before, r), (1, after, r)]:
        first, second = (lists_s[band * 4 + d, e, region] for e in range(2))
        part = points + d * points
        for block in range(blocks):
            bases.append(jnp.where(first == block, part, jnp.where(second == block, part + LANES, FAR)))

    dep_t[...] = jnp.transpose(dep_v[...])
    hw_t[...] = jnp.transpose(hw_v[...])
    stencil = dep_v.shape[0]

    def weigh(i, carry):
        rows_i = pl.ds(pl.multiple_of(i * 16, 16), 16)
        dep, hw = dep_t[rows_i, :], hw_t[rows_i, :]
        lane = lax.broadcasted_iota(jnp.int32, (8, LANES), 1)
        sides = []
        for s in range(2):
            deps = [jnp.broadcast_to(dep[s * 8 : s * 8 + 8, c : c + 1], (8, LANES)) for c in range(stencil)]
            hws = [jnp.broadcast_to(hw[s * 8 : s * 8 + 8, c : c + 1], (8, LANES)) for c in range(stencil)]
            totals = []
            for base in bases:
                target = lane + base
                total = jnp.where(deps[0] == target, hws[0], 0.0)
                for c in range(1, stencil):
                    total = total + jnp.where(deps[c] == target, hws[c], 0.0)
                totals.append(total)
            sides.append(totals)
        for j in range(len(bases)):
            hi, lo = halves(jnp.concatenate([sides[0][j], sides[1][j]], axis=0))
            w_hi[rows_i, j * LANES : (j + 1) * LANES] = hi
            w_lo[rows_i, j * LANES : (j + 1) * LANES] = lo
        return carry

    lax.fori_loop(0, points // 16, weigh, 0, unroll=4)

    @pl.when(spot == gate)
    def _():
        pl.semaphore_wait(gate_sem, planes - 1)
        for i in range(1, plane):
            signal(plane_sem, b, plane_mate(i))

    for load in loads[3:]:
        load.wait()
    base_t[...] = jnp.transpose(base_v[...])
    for m in range(4):
        vw_t[m] = jnp.transpose(vw_v[m])
    v_hi, v_lo = halves(vop_v[...])
    v_cat = jnp.concatenate([jnp.concatenate([v, v], axis=1) for v in (v_hi, v_lo)], axis=0)

    def product(first, last):
        both = jnp.dot(w_hi[:, first:last], e_cat[first:last, :], preferred_element_type=F32)
        rest = jnp.dot(w_lo[:, first:last], e_cat[first:last, :LEV], preferred_element_type=F32)
        return both[:, :LEV] + both[:, LEV:] + rest

    def one_field(t, carry):
        f = field_of(r, t)
        column = pl.multiple_of(f * LEV, LEV)
        near = 3 * points
        e_cat[:points, :LEV], e_cat[:points, LEV:] = halves(own[:, pl.ds(column, LEV)])
        for d in (2, 3):
            halo_copy(t, d, b, r).wait_recv()
            part = slice((d - 1) * points, d * points)
            e_cat[part, :LEV], e_cat[part, LEV:] = halves(halo[t, d])
        near_sum[...] = product(0, near)

        @pl.when(b > 0)
        def _():
            halo_copy(t, 0, b, r).wait_recv()

        @pl.when(b < bands - 1)
        def _():
            halo_copy(t, 1, b, r).wait_recv()

        for d in (0, 1):
            part = slice((d + 3) * points, (d + 4) * points)
            e_cat[part, :LEV], e_cat[part, LEV:] = halves(halo[t, d])
        horizontal = near_sum[...] + product(near, 5 * points)
        mixed = jnp.zeros((points, LEV), F32)
        for m in range(4):
            picked = jnp.take_along_axis(horizontal, base_t[...] + (m - 1), axis=1, mode="promise_in_bounds")
            mixed = mixed + vw_t[m] * picked
        i_hi, i_lo = halves(mixed)
        i_cat = jnp.concatenate([i_hi, i_lo], axis=1)
        operated = lax.dot_general(v_cat, i_cat, NT, preferred_element_type=F32)
        made[t] = operated[:LEV] + operated[LEV:]

        @pl.when((t == 0) & (spot != gate))
        def _():
            pl.semaphore_wait(plane_sem, 1)

        place = pl.ds(pl.multiple_of(r * points, points), points)

        def send_rows(step, carry):
            i = step // 2 + lax.rem(step, 2) * (group // 2)
            target = f * group + i
            src = made.at[t, pl.ds(pl.multiple_of(i * rows, rows), rows)]
            dst = out.at[:, place]

            @pl.when(target != r)
            def _():
                pltpu.make_async_remote_copy(
                    src_ref=src,
                    dst_ref=dst,
                    send_sem=send_sem,
                    recv_sem=recv_sem,
                    device_id=(b, target),
                    device_id_type=MESH,
                ).start()

            @pl.when(target == r)
            def _():
                pltpu.make_async_copy(src, dst, own_sem).start()

            return carry

        lax.fori_loop(0, group, send_rows, 0)
        return carry

    lax.fori_loop(0, n_fields, one_field, 0)

    def halo_sent(t, carry):
        @pl.when(b < bands - 1)
        def _():
            halo_copy(t, 0, b, r).wait_send()

        @pl.when(b > 0)
        def _():
            halo_copy(t, 1, b, r).wait_send()

        halo_copy(t, 2, b, east).wait_send()
        halo_copy(t, 3, b, west).wait_send()
        return carry

    lax.fori_loop(0, n_fields, halo_sent, 0)
    mine = out.at[:, :points]
    pltpu.make_async_copy(mine, mine, own_sem).wait()
    others = out.at[:, : (regions - 1) * points]
    pltpu.make_async_copy(others, others, send_sem).wait()
    pltpu.make_async_copy(others, others, recv_sem).wait()


def solution(mesh):
    bands, regions = mesh.shape["band"], mesh.shape["region"]

    def body(fields, send_list, departure, hweight, base_level, vweight, vertical_op):
        points, width = fields.shape
        n_fields = width // LEV
        stencil = departure.shape[0]
        lists = send_list.transpose(0, 2, 3, 1).reshape(bands * 4, 2, regions)
        extended = points * 5
        anywhere = pl.BlockSpec(memory_space=pl.ANY)
        rows = width // regions
        return pl.pallas_call(
            functools.partial(kernel, bands, regions),
            out_shape=pltpu.VMEM((rows, points * regions), F32),
            in_specs=[anywhere] * 7,
            out_specs=anywhere,
            scratch_shapes=[
                pltpu.VMEM((points, width), F32),
                pltpu.VMEM((n_fields, 4, points, LEV), F32),
                pltpu.SMEM(lists.shape, jnp.int32),
                pltpu.VMEM(departure.shape, jnp.int32),
                pltpu.VMEM(hweight.shape, F32),
                pltpu.VMEM(base_level.shape, jnp.int32),
                pltpu.VMEM(vweight.shape, F32),
                pltpu.VMEM(vertical_op.shape, F32),
                pltpu.VMEM((points, stencil), jnp.int32),
                pltpu.VMEM((points, stencil), F32),
                pltpu.VMEM((points, extended), BF16),
                pltpu.VMEM((points, extended), BF16),
                pltpu.VMEM((extended, 2 * LEV), BF16),
                pltpu.VMEM((points, LEV), jnp.int32),
                pltpu.VMEM((4, points, LEV), F32),
                pltpu.VMEM((n_fields, LEV, points), F32),
                pltpu.VMEM((points, LEV), F32),
                pltpu.SemaphoreType.DMA((7,)),
                pltpu.SemaphoreType.DMA((n_fields, 4)),
                pltpu.SemaphoreType.DMA((n_fields, 4)),
                pltpu.SemaphoreType.DMA,
                pltpu.SemaphoreType.DMA,
                pltpu.SemaphoreType.DMA,
                pltpu.SemaphoreType.REGULAR,
                pltpu.SemaphoreType.REGULAR,
            ],
            compiler_params=pltpu.CompilerParams(
                collective_id=0, has_side_effects=True, vmem_limit_bytes=32 * 2**20
            ),
            name="semi_lagrangian",
        )(*[pltpu.with_memory_space_constraint(a, pltpu.HBM) for a in (fields, lists, departure, hweight, base_level, vweight, vertical_op)])

    points_last = P(None, ("band", "region"))
    return jax.shard_map(
        body,
        mesh=mesh,
        in_specs=(
            P(("band", "region"), None),
            P(),
            points_last,
            points_last,
            points_last,
            P(None, None, ("band", "region")),
            P(),
        ),
        out_specs=P("region", "band"),
        check_vma=False,
    )
```
